512 devices in a mesh: px: 32 (over x, z_lo), py: 16 (over y, z_hi, core).
Axes of the slice: x: 4, y: 4, z: 16 (z_hi: 2, z_lo: 8; z = z_hi * 8 + z_lo), core: 2. Of those that a mesh axis runs over, the one named last changes fastest.
Arguments:
- start_field: float32 [512, 512, 256], P('px', 'py'), may hold values from 0.25 to 4
- end_adjoint: float32 [512, 512, 256], P('px', 'py'), may hold values from 0.25 to 4
- potential: float32 [512, 512, 256], P('px', 'py'), may hold values from -15 to 15
- line_xy: float32 [512, 512], replicated, may hold values from -1 to 2
- line_z: float32 [256, 256], replicated, may hold values from -1 to 2
Outputs:
- final_field: float32 [512, 512, 256], P('px', 'py')
- first_adjoint: float32 [512, 512, 256], P('px', 'py')
- density: float32 [512, 512, 256], P('px', 'py')
The draws below stay inside these ranges and needn't reach their ends.
All inputs are finite; a program needn't handle non-finite values.
Results may differ from the reference program's by a relative error of at most 0.0001.
Values sent between devices are 32-bit elements; how exact they have to be, the bound alone decides.
A program may use at most 64 MiB of HBM per device.

```python
import math
import jax
import jax.numpy as jnp
from jax import lax

NX = 512
NZ = 256
STEPS = 1


def draw_line_xy(key, part):
    key = jax.random.fold_in(key, 11)
    rows = jnp.arange(NX)[:, None]
    columns = jnp.arange(NX)[None, :]
    identity = jnp.where(rows == columns, 1.0, 0.0).astype(jnp.float32)
    noise = jnp.clip(jax.random.normal(key, (NX, NX), jnp.float32), -3.0, 3.0)
    return identity + 0.5 / NX ** 0.5 * noise


def draw_line_z(key, part):
    key = jax.random.fold_in(key, 23)
    rows = jnp.arange(NZ)[:, None]
    columns = jnp.arange(NZ)[None, :]
    identity = jnp.where(rows == columns, 1.0, 0.0).astype(jnp.float32)
    noise = jnp.clip(jax.random.normal(key, (NZ, NZ), jnp.float32), -3.0, 3.0)
    return identity + 0.5 / NZ ** 0.5 * noise


def block_levels(key, shape, shards, low, largest):
    def one(position, shards_of):
        steps = jax.random.uniform(jax.random.fold_in(jax.random.fold_in(key, 6), position), (shards_of,), jnp.float32, low / len(shards), largest / len(shards))
        return jnp.repeat(jnp.exp(steps), shape[position] // shards_of).reshape((-1,) + (1,) * (len(shape) - position - 1))

    level = one(*shards[0])
    for cut in shards[1:]:
        level = level * one(*cut)
    return level


def bell_draw(stream_key, shape, deviation, bound, pieces=(), kind=jnp.bfloat16):
    factor_of = block_levels(stream_key, shape, pieces, -0.22, 0.18) if pieces else 1.0
    array = jax.random.normal(stream_key, shape, jnp.float32) * deviation * factor_of
    return jnp.minimum(jnp.maximum(array, -bound), bound).astype(kind)


def setup_inputs(seed: int = 0) -> dict:
    seeds = jax.random.split(jax.random.key(seed), 6)
    start_field = jnp.clip(jnp.exp(math.log(4.0) - 2.7725887 * jax.random.uniform(seeds[0], (NX, NX, NZ), jnp.float32) ** block_levels(seeds[0], (NX, NX, NZ), ((0, 32), (1, 16)), -0.2, 0.2)), 0.25, 4.0)
    end_adjoint = jnp.clip(jnp.exp(math.log(4.0) - 2.7725887 * jax.random.uniform(seeds[1], (NX, NX, NZ), jnp.float32) ** block_levels(seeds[1], (NX, NX, NZ), ((0, 32), (1, 16)), -0.2, 0.2)), 0.25, 4.0)
    potential = bell_draw(seeds[2], (NX, NX, NZ), 3.0, 15.0, ((0, 32), (1, 16)), jnp.float32)
    line_xy = draw_line_xy(jax.random.fold_in(seeds[5], 71), 0)
    line_z = draw_line_z(jax.random.fold_in(seeds[5], 71), 0)
    return {"start_field": start_field, "end_adjoint": end_adjoint, "potential": potential, "line_xy": line_xy, "line_z": line_z}


def along(field, matrix, axis):
    if axis == 0:
        return jnp.einsum('jbc,ij->ibc', field, matrix, precision=lax.Precision.HIGHEST)
    if axis == 1:
        return jnp.einsum('ajc,ij->aic', field, matrix, precision=lax.Precision.HIGHEST)
    return jnp.einsum('abj,ij->abi', field, matrix, precision=lax.Precision.HIGHEST)


def propagate(field, half, line_xy, line_z, adjoint):
    matrix_xy = line_xy.T if adjoint else line_xy
    matrix_z = line_z.T if adjoint else line_z
    moved = half * field
    moved = along(moved, matrix_z, 2)
    moved = along(moved, matrix_xy, 1)
    moved = along(moved, matrix_xy, 0)
    return half * moved


def reference(start_field, end_adjoint, potential, line_xy, line_z):
    half = jnp.exp(-0.05 * potential)
    forward_list = [start_field]
    for index in range(STEPS):
        forward_list.append(propagate(forward_list[-1], half, line_xy, line_z, False))
    adjoint_list = [end_adjoint]
    for index in range(STEPS):
        adjoint_list.append(propagate(adjoint_list[-1], half, line_xy, line_z, True))
    adjoint_list = adjoint_list[::-1]
    density = jnp.zeros_like(start_field)
    for index in range(STEPS + 1):
        weight = 0.5 if index == 0 or index == STEPS else 1.0
        density = density + (0.1 * weight) * forward_list[index] * adjoint_list[index]
    return forward_list[-1], adjoint_list[0], density
```

```python
import functools
import jax
import jax.numpy as jnp
from jax import lax
from jax.sharding import PartitionSpec as P
from jax.experimental import pallas as pl
from jax.experimental.pallas import tpu as pltpu

MESH = pl.DeviceIdType.MESH
F32 = jnp.float32
BF16 = jnp.bfloat16
NX_CHIPS, NY_CHIPS, NZ_CHIPS = 4, 4, 16


def split(value):
    high = value.astype(BF16)
    return high, (value - high.astype(F32)).astype(BF16)


def contract(left, right, dims):
    return lax.dot_general(left, right, (dims, ((), ())), preferred_element_type=F32)


NN = ((1,), (0,))
NT = ((1,), (1,))


def contract3(left, right, dims):
    (left_high, left_low), (right_high, right_low) = left, right
    return contract(left_high, right_high, dims) + (
        contract(left_high, right_low, dims) + contract(left_low, right_high, dims)
    )


def kernel(
    start_hbm, end_hbm, potential_hbm, xy_hbm, z_hbm,
    final_hbm, first_hbm, density_hbm,
    field, half, pot, xy, lz, result,
    send_z, got_z, gather_x, gather_y, part_send, part_got, part_own, send_back, got_back,
    weight_x, weight_y,
    in_sem, out_sem, z_send_sem, z_recv_sem, x_send_sem, x_recv_sem, y_send_sem, y_recv_sem,
    c_send_sem, c_recv_sem, b_send_sem, b_recv_sem,
):
    px, py = lax.axis_index("px"), lax.axis_index("py")
    x, z_low = px // 8, px % 8
    y, z_high, core = py // 4, (py // 2) % 2, py % 2
    z = z_high * 8 + z_low

    def device(x_at, y_at, z_at, core_at):
        return {"px": x_at * 8 + z_at % 8, "py": y_at * 4 + (z_at // 8) * 2 + core_at}

    loads = [
        pltpu.make_async_copy(source, target, in_sem.at[i])
        for i, (source, target) in enumerate(
            [(potential_hbm, pot), (start_hbm, field.at[0]), (z_hbm, lz), (xy_hbm, xy), (end_hbm, field.at[1])]
        )
    ]
    for load in loads:
        load.start()
    barrier = pltpu.get_barrier_semaphore()

    def signal(target):
        pl.semaphore_signal(barrier, inc=1, device_id=target, device_id_type=MESH)

    @pl.loop(1, NZ_CHIPS)
    def _(step):
        signal(device(x, y, (z + step) % NZ_CHIPS, core))

    for step in range(1, 4):
        signal(device((x + step) % 4, y, z, core))
        signal(device(x, (y + step) % 4, z, core))
    signal(device(x, y, z, 1 - core))

    def exchange_z(source, target, send_sem, recv_sem, chunk):
        @pl.loop(1, NZ_CHIPS)
        def _(step):
            peer = (z + step) % NZ_CHIPS
            pltpu.make_async_remote_copy(
                source.at[chunk, pl.ds(pl.multiple_of(peer * 32, 32), 32)],
                target.at[chunk, pl.ds(pl.multiple_of(z * 32, 32), 32)],
                send_sem.at[chunk], recv_sem.at[chunk],
                device_id=device(x, y, peer, core), device_id_type=MESH,
            ).start()

        mine = pl.ds(pl.multiple_of(z * 32, 32), 32)
        pltpu.make_async_copy(source.at[chunk, mine], target.at[chunk, mine], recv_sem.at[chunk]).start()

    def wait_z(target, recv_sem, chunk):
        pltpu.make_async_copy(target.at[chunk], target.at[chunk], recv_sem.at[chunk]).wait()

    def wait_z_sent(source, send_sem, chunk):
        sent = source.at[chunk, pl.ds(0, 480)]
        pltpu.make_async_copy(sent, sent, send_sem.at[chunk]).wait()

    def ring_copies(buffer, send_sem, recv_sem, chunk, axis):
        here = x if axis == 0 else y
        copies = []
        for step in (1, 3, 2):
            there = (here + step) % 4
            target = device(there, y, z, core) if axis == 0 else device(x, there, z, core)
            copies.append(
                pltpu.make_async_remote_copy(
                    buffer.at[chunk, here], buffer.at[chunk, here],
                    send_sem.at[chunk, step - 1], recv_sem.at[chunk, step - 1],
                    device_id=target, device_id_type=MESH,
                )
            )
        return copies

    def core_copy(chunk):
        return pltpu.make_async_remote_copy(
            part_send.at[chunk], part_got.at[chunk], c_send_sem.at[chunk], c_recv_sem.at[chunk],
            device_id=device(x, y, z, 1 - core), device_id_type=MESH,
        )

    lane = lax.broadcasted_iota(jnp.int32, (8, 128), 1)
    low_64 = lane % 128 < 64
    low_32 = lane % 64 < 32

    def regroup(a, b, c, d):
        a, c = jnp.where(low_64, a, pltpu.roll(c, 64, 1)), jnp.where(low_64, pltpu.roll(a, 64, 1), c)
        b, d = jnp.where(low_64, b, pltpu.roll(d, 64, 1)), jnp.where(low_64, pltpu.roll(b, 64, 1), d)
        a, b = jnp.where(low_32, a, pltpu.roll(b, 32, 1)), jnp.where(low_32, pltpu.roll(a, 96, 1), b)
        c, d = jnp.where(low_32, c, pltpu.roll(d, 32, 1)), jnp.where(low_32, pltpu.roll(c, 96, 1), d)
        return a, b, c, d

    def step_z(chunk, line, values):
        value = contract3(line, values, NT)
        for at in range(16):
            for tile in range(4):
                send_z[chunk, pl.ds(at * 32 + tile * 8, 8)] = value[at * 8 : at * 8 + 8, tile * 128 : tile * 128 + 128]

    def step_z_send(chunk):
        exchange_z(send_z, got_z, z_send_sem, z_recv_sem, chunk)

    def step_x_send(chunk):
        wait_z(got_z, z_recv_sem, chunk)
        for pair in range(4):
            for tile in range(4):
                parts = [
                    got_z[chunk, pl.ds(high * 256 + tile * 8 + pair * 2 + p, 8, stride=32), :]
                    for p in range(2) for high in range(2)
                ]
                for i, part in enumerate(regroup(*parts)):
                    gather_x[chunk, x, pl.ds((tile * 4 + i) * 8, 8), pl.ds(pair * 128, 128)] = part
        for copy in ring_copies(gather_x, x_send_sem, x_recv_sem, chunk, 0):
            copy.start()

    def step_y_send(chunk):
        kind = chunk // 2
        for copy in ring_copies(gather_x, x_send_sem, x_recv_sem, chunk, 0):
            copy.wait_recv()
        values = split(gather_x[chunk].reshape(512, 512))
        gather_y[chunk, y] = contract3((weight_x[kind, 0], weight_x[kind, 1]), values, NN)
        for copy in ring_copies(gather_y, y_send_sem, y_recv_sem, chunk, 1):
            copy.start()

    def step_core_send(chunk):
        kind = chunk // 2
        for copy in ring_copies(gather_y, y_send_sem, y_recv_sem, chunk, 1):
            copy.wait_recv()
        weights = (weight_y[kind, 0], weight_y[kind, 1])
        for pair in range(4):
            lanes = pl.ds(pair * 128, 128)
            values = jnp.concatenate([gather_y[chunk, k, :, lanes] for k in range(4)], axis=1)
            out = contract3(split(values), weights, NN)
            part_own[chunk, :, lanes] = out[:, :128]
            part_send[chunk, :, lanes] = out[:, 128:]
        core_copy(chunk).start()

    def step_back(chunk):
        core_copy(chunk).wait_recv()
        for pair in range(4):
            for tile in range(4):
                parts = []
                for i in range(4):
                    at = (chunk, pl.ds((tile * 4 + i) * 8, 8), pl.ds(pair * 128, 128))
                    parts.append(part_own[at] + part_got[at])
                parts = regroup(*parts)
                for p in range(2):
                    for high in range(2):
                        rows = pl.ds(high * 256 + tile * 8 + pair * 2 + p, 8, stride=32)
                        send_back[chunk, rows, :] = parts[p * 2 + high]
        exchange_z(send_back, got_back, b_send_sem, b_recv_sem, chunk)

    def out_copy(chunk, slot, target):
        lanes = pl.ds((chunk % 2) * 128, 128)
        return pltpu.make_async_copy(
            result.at[slot, :, :, lanes], target.at[:, :, lanes], out_sem.at[slot, chunk % 2]
        )

    def step_last(chunk):
        kind = chunk // 2
        lanes = pl.ds((chunk % 2) * 128, 128)
        wait_z(got_back, b_recv_sem, chunk)
        arrived = got_back[chunk].reshape(16, 4, 8, 128)
        value = jnp.concatenate(
            [jnp.transpose(arrived[:, tile].reshape(128, 128)).reshape(4, 32, 128) for tile in range(4)]
        ) * half[:, :, lanes]
        result[kind, :, :, lanes] = value
        if kind == 0:
            out_copy(chunk, 0, final_hbm).start()
        else:
            out_copy(chunk, 1, first_hbm).start()
            result[2, :, :, lanes] = 0.05 * (
                field[0, :, :, lanes] * value + result[0, :, :, lanes] * field[1, :, :, lanes]
            )
            out_copy(chunk, 2, density_hbm).start()

    loads[0].wait()
    loads[1].wait()
    half[...] = jnp.exp(-0.05 * pot[...])
    values = split((half[...] * field[0]).reshape(512, 256))
    loads[2].wait()
    step_z(0, split(lz[:128, :]), values)
    pl.semaphore_wait(barrier, 22)
    step_z_send(0)
    step_z(1, split(lz[128:, :]), values)
    step_z_send(1)

    loads[3].wait()
    loads[4].wait()
    row = lax.broadcasted_iota(jnp.int32, (128, 128), 0)
    column = lax.broadcasted_iota(jnp.int32, (128, 128), 1)
    order_x = (column == (row % 8) * 16 + row // 8).astype(F32).astype(BF16)
    order_y = (column == (row % 64) // 32 * 64 + core * 32 + row % 32).astype(F32).astype(BF16)
    row = lax.broadcasted_iota(jnp.int32, (256, 128), 0)
    column = lax.broadcasted_iota(jnp.int32, (256, 128), 1)
    other = (core + row // 128) % 2
    order_out = (column == (row % 64) // 32 * 64 + other * 32 + row % 32).astype(F32).astype(BF16)
    row = lax.broadcasted_iota(jnp.int32, (128, 256), 0)
    column = lax.broadcasted_iota(jnp.int32, (128, 256), 1)
    same = row // 64 == column % 128 // 64
    at_x = pl.ds(pl.multiple_of(x * 128, 128), 128)
    at_y = pl.ds(pl.multiple_of(y * 128, 128), 128)
    for kind in range(2):
        for k in range(4):
            block = pl.ds(k * 128, 128)
            if kind == 0:
                of_x, of_y = split(xy[at_x, block]), split(xy[at_y, block])
            else:
                of_x, of_y = split(xy[block, at_x]), split(xy[block, at_y])
            for part in range(2):
                turned = contract(order_x, of_x[part], NN if kind == 0 else NT).astype(BF16)
                weight_x[kind, part, :, block] = contract(turned, order_x, NT).astype(BF16)
                turned = contract(order_y, of_y[part], NT if kind == 0 else NN).astype(BF16)
                weight_y[kind, part, block, :] = jnp.where(same, contract(turned, order_out, NT), 0.0).astype(BF16)

    turned = jnp.transpose(lz[...])
    values = split((half[...] * field[1]).reshape(512, 256))
    step_z(2, split(turned[:128, :]), values)
    step_z(3, split(turned[128:, :]), values)

    step_x_send(0)
    step_z_send(2)
    step_x_send(1)
    step_z_send(3)
    step_y_send(0)
    step_x_send(2)
    step_y_send(1)
    step_core_send(0)
    step_x_send(3)
    step_back(0)
    step_y_send(2)
    step_core_send(1)
    step_back(1)
    step_y_send(3)
    step_core_send(2)
    step_back(2)
    step_core_send(3)
    step_back(3)
    for chunk in range(4):
        step_last(chunk)

    for chunk in range(4):
        wait_z_sent(send_z, z_send_sem, chunk)
        wait_z_sent(send_back, b_send_sem, chunk)
        for copy in ring_copies(gather_x, x_send_sem, x_recv_sem, chunk, 0):
            copy.wait_send()
        for copy in ring_copies(gather_y, y_send_sem, y_recv_sem, chunk, 1):
            copy.wait_send()
        core_copy(chunk).wait_send()
    for half_z in range(2):
        out_copy(half_z, 0, final_hbm).wait()
        out_copy(half_z, 1, first_hbm).wait()
        out_copy(half_z, 2, density_hbm).wait()


def body(start_field, end_adjoint, potential, line_xy, line_z):
    shape = start_field.shape
    dma = pltpu.SemaphoreType.DMA
    chunk = (4, 128, 512)
    pieces = (4, 512, 128)
    gather = (4, 4, 128, 512)
    return pl.pallas_call(
        kernel,
        out_shape=[jax.ShapeDtypeStruct(shape, F32)] * 3,
        in_specs=[pl.BlockSpec(memory_space=pl.ANY)] * 5,
        out_specs=[pl.BlockSpec(memory_space=pl.ANY)] * 3,
        scratch_shapes=[
            pltpu.VMEM((2,) + shape, F32),
            pltpu.VMEM(shape, F32),
            pltpu.VMEM(shape, F32),
            pltpu.VMEM(line_xy.shape, F32),
            pltpu.VMEM(line_z.shape, F32),
            pltpu.VMEM((3,) + shape, F32),
            pltpu.VMEM(pieces, F32),
            pltpu.VMEM(pieces, F32),
            pltpu.VMEM(gather, F32),
            pltpu.VMEM(gather, F32),
            pltpu.VMEM(chunk, F32),
            pltpu.VMEM(chunk, F32),
            pltpu.VMEM(chunk, F32),
            pltpu.VMEM(pieces, F32),
            pltpu.VMEM(pieces, F32),
            pltpu.VMEM((2, 2, 128, 512), BF16),
            pltpu.VMEM((2, 2, 512, 256), BF16),
            dma((5,)), dma((3, 2)), dma((4,)), dma((4,)), dma((4, 3)), dma((4, 3)), dma((4, 3)), dma((4, 3)),
            dma((4,)), dma((4,)), dma((4,)), dma((4,)),
        ],
        compiler_params=pltpu.CompilerParams(
            collective_id=0, has_side_effects=True, vmem_limit_bytes=48 * 2**20
        ),
        name="contour_step",
    )(start_field, end_adjoint, potential, line_xy, line_z)


def solution(mesh):
    placed = (P("px", "py", None), P("px", "py", None), P("px", "py", None), P(), P())
    return jax.shard_map(
        body,
        mesh=mesh,
        in_specs=placed,
        out_specs=(P("px", "py", None), P("px", "py", None), P("px", "py", None)),
        check_vma=False,
    )
```

```python
import functools
import jax
import jax.numpy as jnp
from jax import lax
from jax.sharding import PartitionSpec as P
from jax.experimental import pallas as pl
from jax.experimental.pallas import tpu as pltpu

MESH = pl.DeviceIdType.MESH
F32 = jnp.float32
BF16 = jnp.bfloat16
NX_CHIPS, NY_CHIPS, NZ_CHIPS = 4, 4, 16


def split(value):
    high = value.astype(BF16)
    return high, (value - high.astype(F32)).astype(BF16)


def contract(left, right, dims):
    return lax.dot_general(left, right, (dims, ((), ())), preferred_element_type=F32)


NN = ((1,), (0,))
NT = ((1,), (1,))


def contract3(left, right, dims):
    (left_high, left_low), (right_high, right_low) = left, right
    return contract(left_high, right_high, dims) + (
        contract(left_high, right_low, dims) + contract(left_low, right_high, dims)
    )


def kernel(
    start_hbm, end_hbm, potential_hbm, xy_hbm, z_hbm,
    final_out, first_out, density_out,
    field, half, pot, xy, lz,
    send_z, got_z, gather_x, gather_y, part_send, part_got, part_own, send_back, got_back,
    weight_x, weight_y,
    in_sem, z_send_sem, z_recv_sem, x_send_sem, x_recv_sem, y_send_sem, y_recv_sem,
    c_send_sem, c_recv_sem, b_send_sem, b_recv_sem,
):
    px, py = lax.axis_index("px"), lax.axis_index("py")
    x, z_low = px // 8, px % 8
    y, z_high, core = py // 4, (py // 2) % 2, py % 2
    z = z_high * 8 + z_low

    def device(x_at, y_at, z_at, core_at):
        return {"px": x_at * 8 + z_at % 8, "py": y_at * 4 + (z_at // 8) * 2 + core_at}

    loads = [
        pltpu.make_async_copy(source, target, in_sem.at[i])
        for i, (source, target) in enumerate(
            [(potential_hbm, pot), (start_hbm, field.at[0]), (z_hbm, lz), (xy_hbm, xy), (end_hbm, field.at[1])]
        )
    ]
    for load in loads:
        load.start()
    barrier = pltpu.get_barrier_semaphore()

    def signal(target):
        pl.semaphore_signal(barrier, inc=1, device_id=target, device_id_type=MESH)

    @pl.loop(1, NZ_CHIPS)
    def _(step):
        signal(device(x, y, (z + step) % NZ_CHIPS, core))

    for step in range(1, 4):
        signal(device((x + step) % 4, y, z, core))
        signal(device(x, (y + step) % 4, z, core))
    signal(device(x, y, z, 1 - core))

    def exchange_z(source, target, send_sem, recv_sem, chunk):
        @pl.loop(1, NZ_CHIPS)
        def _(step):
            peer = (z + step) % NZ_CHIPS
            pltpu.make_async_remote_copy(
                source.at[chunk, pl.ds(pl.multiple_of(peer * 32, 32), 32)],
                target.at[chunk, pl.ds(pl.multiple_of(z * 32, 32), 32)],
                send_sem.at[chunk], recv_sem.at[chunk],
                device_id=device(x, y, peer, core), device_id_type=MESH,
            ).start()

        mine = pl.ds(pl.multiple_of(z * 32, 32), 32)
        pltpu.make_async_copy(source.at[chunk, mine], target.at[chunk, mine], recv_sem.at[chunk]).start()

    def wait_z(target, recv_sem, chunk):
        pltpu.make_async_copy(target.at[chunk], target.at[chunk], recv_sem.at[chunk]).wait()

    def wait_z_sent(source, send_sem, chunk):
        sent = source.at[chunk, pl.ds(0, 480)]
        pltpu.make_async_copy(sent, sent, send_sem.at[chunk]).wait()

    def ring_copies(buffer, send_sem, recv_sem, chunk, axis):
        here = x if axis == 0 else y
        copies = []
        for step in (1, 3, 2):
            there = (here + step) % 4
            target = device(there, y, z, core) if axis == 0 else device(x, there, z, core)
            copies.append(
                pltpu.make_async_remote_copy(
                    buffer.at[chunk, here], buffer.at[chunk, here],
                    send_sem.at[chunk, step - 1], recv_sem.at[chunk, step - 1],
                    device_id=target, device_id_type=MESH,
                )
            )
        return copies

    def core_copy(chunk):
        return pltpu.make_async_remote_copy(
            part_send.at[chunk], part_got.at[chunk], c_send_sem.at[chunk], c_recv_sem.at[chunk],
            device_id=device(x, y, z, 1 - core), device_id_type=MESH,
        )

    lane = lax.broadcasted_iota(jnp.int32, (8, 128), 1)
    low_64 = lane % 128 < 64
    low_32 = lane % 64 < 32

    def regroup(a, b, c, d):
        a, c = jnp.where(low_64, a, pltpu.roll(c, 64, 1)), jnp.where(low_64, pltpu.roll(a, 64, 1), c)
        b, d = jnp.where(low_64, b, pltpu.roll(d, 64, 1)), jnp.where(low_64, pltpu.roll(b, 64, 1), d)
        a, b = jnp.where(low_32, a, pltpu.roll(b, 32, 1)), jnp.where(low_32, pltpu.roll(a, 96, 1), b)
        c, d = jnp.where(low_32, c, pltpu.roll(d, 32, 1)), jnp.where(low_32, pltpu.roll(c, 96, 1), d)
        return a, b, c, d

    def step_z(chunk, line, values):
        value = contract3(line, values, NT)
        for at in range(16):
            for tile in range(4):
                send_z[chunk, pl.ds(at * 32 + tile * 8, 8)] = value[at * 8 : at * 8 + 8, tile * 128 : tile * 128 + 128]

    def step_z_send(chunk):
        exchange_z(send_z, got_z, z_send_sem, z_recv_sem, chunk)

    def step_x_send(chunk):
        wait_z(got_z, z_recv_sem, chunk)
        for pair in range(4):
            for tile in range(4):
                parts = [
                    got_z[chunk, pl.ds(high * 256 + tile * 8 + pair * 2 + p, 8, stride=32), :]
                    for p in range(2) for high in range(2)
                ]
                for i, part in enumerate(regroup(*parts)):
                    gather_x[chunk, x, pl.ds((tile * 4 + i) * 8, 8), pl.ds(pair * 128, 128)] = part
        for copy in ring_copies(gather_x, x_send_sem, x_recv_sem, chunk, 0):
            copy.start()

    def step_y_send(chunk):
        kind = chunk // 2
        for copy in ring_copies(gather_x, x_send_sem, x_recv_sem, chunk, 0):
            copy.wait_recv()
        values = split(gather_x[chunk].reshape(512, 512))
        gather_y[chunk, y] = contract3((weight_x[kind, 0], weight_x[kind, 1]), values, NN)
        for copy in ring_copies(gather_y, y_send_sem, y_recv_sem, chunk, 1):
            copy.start()

    def step_core_send(chunk):
        kind = chunk // 2
        for copy in ring_copies(gather_y, y_send_sem, y_recv_sem, chunk, 1):
            copy.wait_recv()
        weights = (weight_y[kind, 0], weight_y[kind, 1])
        for pair in range(4):
            lanes = pl.ds(pair * 128, 128)
            values = jnp.concatenate([gather_y[chunk, k, :, lanes] for k in range(4)], axis=1)
            out = contract3(split(values), weights, NN)
            part_own[chunk, :, lanes] = out[:, :128]
            part_send[chunk, :, lanes] = out[:, 128:]
        core_copy(chunk).start()

    def step_back(chunk):
        core_copy(chunk).wait_recv()
        for pair in range(4):
            for tile in range(4):
                parts = []
                for i in range(4):
                    at = (chunk, pl.ds((tile * 4 + i) * 8, 8), pl.ds(pair * 128, 128))
                    parts.append(part_own[at] + part_got[at])
                parts = regroup(*parts)
                for p in range(2):
                    for high in range(2):
                        rows = pl.ds(high * 256 + tile * 8 + pair * 2 + p, 8, stride=32)
                        send_back[chunk, rows, :] = parts[p * 2 + high]
        exchange_z(send_back, got_back, b_send_sem, b_recv_sem, chunk)

    def step_last(chunk):
        kind = chunk // 2
        lanes = pl.ds((chunk % 2) * 128, 128)
        wait_z(got_back, b_recv_sem, chunk)
        arrived = got_back[chunk].reshape(16, 4, 8, 128)
        value = jnp.concatenate(
            [jnp.transpose(arrived[:, tile].reshape(128, 128)).reshape(4, 32, 128) for tile in range(4)]
        ) * half[:, :, lanes]
        if kind == 0:
            final_out[:, :, lanes] = value
        else:
            first_out[:, :, lanes] = value
            density_out[:, :, lanes] = 0.05 * (
                field[0, :, :, lanes] * value + final_out[:, :, lanes] * field[1, :, :, lanes]
            )

    loads[0].wait()
    loads[1].wait()
    half[...] = jnp.exp(-0.05 * pot[...])
    values = split((half[...] * field[0]).reshape(512, 256))
    loads[2].wait()
    step_z(0, split(lz[:128, :]), values)
    pl.semaphore_wait(barrier, 22)
    step_z_send(0)
    step_z(1, split(lz[128:, :]), values)
    step_z_send(1)

    loads[3].wait()
    loads[4].wait()
    row = lax.broadcasted_iota(jnp.int32, (128, 128), 0)
    column = lax.broadcasted_iota(jnp.int32, (128, 128), 1)
    order_x = (column == (row % 8) * 16 + row // 8).astype(F32).astype(BF16)
    order_y = (column == (row % 64) // 32 * 64 + core * 32 + row % 32).astype(F32).astype(BF16)
    row = lax.broadcasted_iota(jnp.int32, (256, 128), 0)
    column = lax.broadcasted_iota(jnp.int32, (256, 128), 1)
    other = (core + row // 128) % 2
    order_out = (column == (row % 64) // 32 * 64 + other * 32 + row % 32).astype(F32).astype(BF16)
    row = lax.broadcasted_iota(jnp.int32, (128, 256), 0)
    column = lax.broadcasted_iota(jnp.int32, (128, 256), 1)
    same = row // 64 == column % 128 // 64
    at_x = pl.ds(pl.multiple_of(x * 128, 128), 128)
    at_y = pl.ds(pl.multiple_of(y * 128, 128), 128)
    for kind in range(2):
        for k in range(4):
            block = pl.ds(k * 128, 128)
            if kind == 0:
                of_x, of_y = split(xy[at_x, block]), split(xy[at_y, block])
            else:
                of_x, of_y = split(xy[block, at_x]), split(xy[block, at_y])
            for part in range(2):
                turned = contract(order_x, of_x[part], NN if kind == 0 else NT).astype(BF16)
                weight_x[kind, part, :, block] = contract(turned, order_x, NT).astype(BF16)
                turned = contract(order_y, of_y[part], NT if kind == 0 else NN).astype(BF16)
                weight_y[kind, part, block, :] = jnp.where(same, contract(turned, order_out, NT), 0.0).astype(BF16)

    turned = jnp.transpose(lz[...])
    values = split((half[...] * field[1]).reshape(512, 256))
    step_z(2, split(turned[:128, :]), values)
    step_z(3, split(turned[128:, :]), values)

    step_x_send(0)
    step_z_send(2)
    step_x_send(1)
    step_z_send(3)
    step_y_send(0)
    step_x_send(2)
    step_y_send(1)
    step_core_send(0)
    step_x_send(3)
    step_back(0)
    step_y_send(2)
    step_core_send(1)
    step_back(1)
    step_y_send(3)
    step_core_send(2)
    step_back(2)
    step_core_send(3)
    step_back(3)
    for chunk in range(4):
        step_last(chunk)

    for chunk in range(4):
        wait_z_sent(send_z, z_send_sem, chunk)
        wait_z_sent(send_back, b_send_sem, chunk)
        for copy in ring_copies(gather_x, x_send_sem, x_recv_sem, chunk, 0):
            copy.wait_send()
        for copy in ring_copies(gather_y, y_send_sem, y_recv_sem, chunk, 1):
            copy.wait_send()
        core_copy(chunk).wait_send()


def store(*refs):
    sources, targets, sem = refs[:3], refs[3:6], refs[6]
    copies = [pltpu.make_async_copy(a, b, sem.at[i]) for i, (a, b) in enumerate(zip(sources, targets))]
    for copy in copies:
        copy.start()
    for copy in copies:
        copy.wait()


def in_hbm(array):
    return pltpu.with_memory_space_constraint(array, pltpu.HBM)


def body(start_field, end_adjoint, potential, line_xy, line_z):
    shape = start_field.shape
    dma = pltpu.SemaphoreType.DMA
    chunk = (4, 128, 512)
    pieces = (4, 512, 128)
    gather = (4, 4, 128, 512)
    outs = pl.pallas_call(
        kernel,
        out_shape=[jax.ShapeDtypeStruct(shape, F32)] * 3,
        in_specs=[pl.BlockSpec(memory_space=pl.ANY)] * 5,
        out_specs=[pl.BlockSpec(memory_space=pltpu.VMEM)] * 3,
        scratch_shapes=[
            pltpu.VMEM((2,) + shape, F32),
            pltpu.VMEM(shape, F32),
            pltpu.VMEM(shape, F32),
            pltpu.VMEM(line_xy.shape, F32),
            pltpu.VMEM(line_z.shape, F32),
            pltpu.VMEM(pieces, F32),
            pltpu.VMEM(pieces, F32),
            pltpu.VMEM(gather, F32),
            pltpu.VMEM(gather, F32),
            pltpu.VMEM(chunk, F32),
            pltpu.VMEM(chunk, F32),
            pltpu.VMEM(chunk, F32),
            pltpu.VMEM(pieces, F32),
            pltpu.VMEM(pieces, F32),
            pltpu.VMEM((2, 2, 128, 512), BF16),
            pltpu.VMEM((2, 2, 512, 256), BF16),
            dma((5,)), dma((4,)), dma((4,)), dma((4, 3)), dma((4, 3)), dma((4, 3)), dma((4, 3)),
            dma((4,)), dma((4,)), dma((4,)), dma((4,)),
        ],
        compiler_params=pltpu.CompilerParams(
            collective_id=0, has_side_effects=True, vmem_limit_bytes=48 * 2**20
        ),
        name="contour_step",
    )(in_hbm(start_field), in_hbm(end_adjoint), in_hbm(potential), in_hbm(line_xy), in_hbm(line_z))
    return pl.pallas_call(
        store,
        out_shape=[jax.ShapeDtypeStruct(shape, F32)] * 3,
        in_specs=[pl.BlockSpec(memory_space=pl.ANY)] * 3,
        out_specs=[pl.BlockSpec(memory_space=pl.ANY)] * 3,
        scratch_shapes=[dma((3,))],
        compiler_params=pltpu.CompilerParams(vmem_limit_bytes=8 * 2**20),
        name="store",
    )(*[pltpu.with_memory_space_constraint(out, pltpu.VMEM) for out in outs])


def solution(mesh):
    placed = (P("px", "py", None), P("px", "py", None), P("px", "py", None), P(), P())
    return jax.shard_map(
        body,
        mesh=mesh,
        in_specs=placed,
        out_specs=(P("px", "py", None), P("px", "py", None), P("px", "py", None)),
        check_vma=False,
    )
```

```python
import functools
import jax
import jax.numpy as jnp
from jax import lax
from jax.sharding import PartitionSpec as P
from jax.experimental import pallas as pl
from jax.experimental.pallas import tpu as pltpu

MESH = pl.DeviceIdType.MESH
F32 = jnp.float32
BF16 = jnp.bfloat16
NX_CHIPS, NY_CHIPS, NZ_CHIPS = 4, 4, 16


def split(value):
    high = value.astype(BF16)
    return high, (value - high.astype(F32)).astype(BF16)


def contract(left, right, dims):
    return lax.dot_general(left, right, (dims, ((), ())), preferred_element_type=F32)


NN = ((1,), (0,))
NT = ((1,), (1,))


def stacked(value):
    return jnp.concatenate(split(value), axis=0)


def contract_left(left, right, dims):
    rows = left.shape[0] // 2
    high, low = split(right)
    both = contract(left, high, dims)
    return both[:rows] + (both[rows:] + contract(left[:rows], low, dims))


def kernel(
    start_hbm, end_hbm, potential_hbm, xy_hbm, z_hbm,
    final_out, first_out, density_out,
    field, half, pot, xy, lz,
    send_z, got_z, out_x, in_x, turn_x, home_x, in_y, part_own, part_send, part_got, turn_y, home_y, send_back, got_back,
    weight_x, weight_y,
    in_sem, z_send_sem, z_recv_sem, ring_send_sem, ring_recv_sem,
    c_send_sem, c_recv_sem, b_send_sem, b_recv_sem,
):
    px, py = lax.axis_index("px"), lax.axis_index("py")
    x, z_low = px // 8, px % 8
    y, z_high, core = py // 4, (py // 2) % 2, py % 2
    z = z_high * 8 + z_low

    def device(x_at, y_at, z_at, core_at):
        return {"px": x_at * 8 + z_at % 8, "py": y_at * 4 + (z_at // 8) * 2 + core_at}

    loads = [
        pltpu.make_async_copy(source, target, in_sem.at[i])
        for i, (source, target) in enumerate(
            [(potential_hbm, pot), (start_hbm, field.at[0]), (z_hbm, lz), (xy_hbm, xy), (end_hbm, field.at[1])]
        )
    ]
    for load in loads:
        load.start()
    barrier = pltpu.get_barrier_semaphore()

    def signal(target):
        pl.semaphore_signal(barrier, inc=1, device_id=target, device_id_type=MESH)

    @pl.loop(1, NZ_CHIPS)
    def _(step):
        signal(device(x, y, (z + step) % NZ_CHIPS, core))

    for step in range(1, 4):
        signal(device((x + step) % 4, y, z, core))
        signal(device(x, (y + step) % 4, z, core))
    signal(device(x, y, z, 1 - core))

    def exchange_z(source, target, send_sem, recv_sem, chunk):
        @pl.loop(0, NZ_CHIPS - 1)
        def _(i):
            step = NZ_CHIPS // 2 + i // 2 - (i % 2) * (2 * (i // 2) + 1)
            peer = (z + step) % NZ_CHIPS
            pltpu.make_async_remote_copy(
                source.at[chunk, pl.ds(pl.multiple_of(peer * 32, 32), 32)],
                target.at[chunk, pl.ds(pl.multiple_of(z * 32, 32), 32)],
                send_sem.at[chunk], recv_sem.at[chunk],
                device_id=device(x, y, peer, core), device_id_type=MESH,
            ).start()

        mine = pl.ds(pl.multiple_of(z * 32, 32), 32)
        pltpu.make_async_copy(source.at[chunk, mine], target.at[chunk, mine], recv_sem.at[chunk]).start()

    def wait_z(target, recv_sem, chunk):
        pltpu.make_async_copy(target.at[chunk], target.at[chunk], recv_sem.at[chunk]).wait()

    def wait_z_sent(source, send_sem, chunk):
        sent = source.at[chunk, pl.ds(0, 480)]
        pltpu.make_async_copy(sent, sent, send_sem.at[chunk]).wait()

    exchanges = ((out_x, in_x, 0), (turn_x, home_x, 0), (home_x, in_y, 1), (turn_y, home_y, 1))

    def ring_copies(stage, chunk):
        source, target, axis = exchanges[stage]
        here = x if axis == 0 else y
        copies = []
        for step in (2, 1, 3):
            there = (here + step) % 4
            peer = device(there, y, z, core) if axis == 0 else device(x, there, z, core)
            copies.append(
                pltpu.make_async_remote_copy(
                    source.at[chunk, there], target.at[chunk, here],
                    ring_send_sem.at[stage, chunk, step - 1], ring_recv_sem.at[stage, chunk, step - 1],
                    device_id=peer, device_id_type=MESH,
                )
            )
        return copies

    def ring_start(stage, chunk):
        source, target, axis = exchanges[stage]
        here = x if axis == 0 else y
        for copy in ring_copies(stage, chunk):
            copy.start()
        target[chunk, here] = source[chunk, here]

    def ring_wait(stage, chunk):
        for copy in ring_copies(stage, chunk):
            copy.wait_recv()

    def core_copy(chunk):
        return pltpu.make_async_remote_copy(
            part_send.at[chunk], part_got.at[chunk], c_send_sem.at[chunk], c_recv_sem.at[chunk],
            device_id=device(x, y, z, 1 - core), device_id_type=MESH,
        )

    lane = lax.broadcasted_iota(jnp.int32, (8, 128), 1)
    low_64 = lane % 128 < 64
    low_32 = lane % 64 < 32

    def regroup(a, b, c, d):
        a, c = jnp.where(low_64, a, pltpu.roll(c, 64, 1)), jnp.where(low_64, pltpu.roll(a, 64, 1), c)
        b, d = jnp.where(low_64, b, pltpu.roll(d, 64, 1)), jnp.where(low_64, pltpu.roll(b, 64, 1), d)
        a, b = jnp.where(low_32, a, pltpu.roll(b, 32, 1)), jnp.where(low_32, pltpu.roll(a, 96, 1), b)
        c, d = jnp.where(low_32, c, pltpu.roll(d, 32, 1)), jnp.where(low_32, pltpu.roll(c, 96, 1), d)
        return a, b, c, d

    def step_z(chunk, line, field_values):
        value = contract(line, field_values[0], NT)
        value = value[:128] + (value[128:] + contract(line[:128], field_values[1], NT))
        for at in range(16):
            for tile in range(4):
                send_z[chunk, pl.ds(at * 32 + tile * 8, 8)] = value[at * 8 : at * 8 + 8, tile * 128 : tile * 128 + 128]

    def step_z_send(chunk):
        exchange_z(send_z, got_z, z_send_sem, z_recv_sem, chunk)

    def step_a(chunk):
        wait_z(got_z, z_recv_sem, chunk)
        for pair in range(4):
            for tile in range(4):
                parts = [
                    got_z[chunk, pl.ds(high * 256 + tile * 8 + pair * 2 + p, 8, stride=32), :]
                    for p in range(2) for high in range(2)
                ]
                for i, part in enumerate(regroup(*parts)):
                    out_x[chunk, pair, pl.ds((tile * 4 + i) * 8, 8), :] = part
        ring_start(0, chunk)

    def step_b(chunk):
        ring_wait(0, chunk)
        values = in_x[chunk].reshape(512, 128)
        turn_x[chunk] = contract_left(weight_x[chunk // 2], values, NN).reshape(4, 128, 128)
        ring_start(1, chunk)

    def step_c(chunk):
        ring_wait(1, chunk)
        ring_start(2, chunk)

    def step_d(chunk):
        kind = chunk // 2
        ring_wait(2, chunk)
        values = stacked(jnp.concatenate([in_y[chunk, k] for k in range(4)], axis=1))
        for block in range(4):
            lanes = pl.ds(block * 256, 256)
            out = contract(values, weight_y[kind, 0, :, lanes], NN)
            out = out[:128] + (out[128:] + contract(values[:128], weight_y[kind, 1, :, lanes], NN))
            part_own[chunk, block] = out[:, :128]
            part_send[chunk, block] = out[:, 128:]
        core_copy(chunk).start()

    def step_e(chunk):
        core_copy(chunk).wait_recv()
        turn_y[chunk] = part_own[chunk] + part_got[chunk]
        ring_start(3, chunk)

    def step_f(chunk):
        ring_wait(3, chunk)
        for pair in range(4):
            for tile in range(4):
                parts = regroup(*[home_y[chunk, pair, pl.ds((tile * 4 + i) * 8, 8)] for i in range(4)])
                for p in range(2):
                    for high in range(2):
                        rows = pl.ds(high * 256 + tile * 8 + pair * 2 + p, 8, stride=32)
                        send_back[chunk, rows, :] = parts[p * 2 + high]
        exchange_z(send_back, got_back, b_send_sem, b_recv_sem, chunk)

    def step_last(chunk):
        kind = chunk // 2
        lanes = pl.ds((chunk % 2) * 128, 128)
        wait_z(got_back, b_recv_sem, chunk)
        arrived = got_back[chunk].reshape(16, 4, 8, 128)
        value = jnp.concatenate(
            [jnp.transpose(arrived[:, tile].reshape(128, 128)).reshape(4, 32, 128) for tile in range(4)]
        ) * half[:, :, lanes]
        if kind == 0:
            final_out[:, :, lanes] = value
        else:
            first_out[:, :, lanes] = value
            density_out[:, :, lanes] = 0.05 * (
                field[0, :, :, lanes] * value + final_out[:, :, lanes] * field[1, :, :, lanes]
            )

    loads[0].wait()
    loads[1].wait()
    half[...] = jnp.exp(-0.05 * pot[...])
    values = split((half[...] * field[0]).reshape(512, 256))
    loads[2].wait()
    step_z(0, stacked(lz[:128, :]), values)
    pl.semaphore_wait(barrier, 22)
    step_z_send(0)
    step_z(1, stacked(lz[128:, :]), values)
    step_z_send(1)

    loads[3].wait()
    loads[4].wait()
    row = lax.broadcasted_iota(jnp.int32, (128, 128), 0)
    column = lax.broadcasted_iota(jnp.int32, (128, 128), 1)
    order_x = (column == (row % 8) * 16 + row // 8).astype(F32).astype(BF16)
    order_y = (column == (row % 64) // 32 * 64 + core * 32 + row % 32).astype(F32).astype(BF16)
    row = lax.broadcasted_iota(jnp.int32, (256, 128), 0)
    column = lax.broadcasted_iota(jnp.int32, (256, 128), 1)
    other = (core + row // 128) % 2
    order_out = (column == (row % 64) // 32 * 64 + other * 32 + row % 32).astype(F32).astype(BF16)
    row = lax.broadcasted_iota(jnp.int32, (128, 256), 0)
    column = lax.broadcasted_iota(jnp.int32, (128, 256), 1)
    same = row // 64 == column % 128 // 64
    for kind in range(2):
        for k in range(4):
            block = pl.ds(k * 128, 128)
            parts = split(xy[block, :] if kind == 0 else xy[:, block])
            columns = split(xy[:, block] if kind == 0 else xy[block, :])
            for part in range(2):
                rows = pl.ds(part * 512 + k * 128, 128)
                turned = contract(order_x, parts[part], NN if kind == 0 else NT).astype(BF16)
                for i in range(4):
                    at = slice(i * 128, i * 128 + 128)
                    weight_x[kind, rows, at] = contract(turned[:, at], order_x, NT).astype(BF16)
                turned = contract(order_y, columns[part], NT if kind == 0 else NN).astype(BF16)
                for i in range(4):
                    value = contract(turned[:, i * 128 : i * 128 + 128], order_out, NT)
                    weight_y[kind, part, block, pl.ds(i * 256, 256)] = jnp.where(same, value, 0.0).astype(BF16)

    turned = jnp.transpose(lz[...])
    values = split((half[...] * field[1]).reshape(512, 256))
    step_z(2, stacked(turned[:128, :]), values)
    step_z(3, stacked(turned[128:, :]), values)

    step_z_send(2)
    step_z_send(3)
    step_a(0)
    step_b(0)
    step_c(0)
    step_a(1)
    step_d(0)
    step_b(1)
    step_e(0)
    step_c(1)
    step_f(0)
    step_a(2)
    step_d(1)
    step_e(1)
    step_b(2)
    step_f(1)
    step_c(2)
    step_a(3)
    step_d(2)
    step_b(3)
    step_e(2)
    step_c(3)
    step_f(2)
    step_d(3)
    step_e(3)
    step_f(3)
    for chunk in range(3):
        step_last(chunk)

    for chunk in range(4):
        wait_z_sent(send_z, z_send_sem, chunk)
        for stage in range(4):
            for copy in ring_copies(stage, chunk):
                copy.wait_send()
        core_copy(chunk).wait_send()
        if chunk < 3:
            wait_z_sent(send_back, b_send_sem, chunk)
    step_last(3)
    wait_z_sent(send_back, b_send_sem, 3)


def store(*refs):
    sources, targets, sem = refs[:3], refs[3:6], refs[6]
    copies = [pltpu.make_async_copy(a, b, sem.at[i]) for i, (a, b) in enumerate(zip(sources, targets))]
    for copy in copies:
        copy.start()
    for copy in copies:
        copy.wait()


def in_hbm(array):
    return pltpu.with_memory_space_constraint(array, pltpu.HBM)


def body(start_field, end_adjoint, potential, line_xy, line_z):
    shape = start_field.shape
    dma = pltpu.SemaphoreType.DMA
    pieces = (4, 512, 128)
    parts = (4, 4, 128, 128)
    outs = pl.pallas_call(
        kernel,
        out_shape=[jax.ShapeDtypeStruct(shape, F32)] * 3,
        in_specs=[pl.BlockSpec(memory_space=pl.ANY)] * 5,
        out_specs=[pl.BlockSpec(memory_space=pltpu.VMEM)] * 3,
        scratch_shapes=[
            pltpu.VMEM((2,) + shape, F32),
            pltpu.VMEM(shape, F32),
            pltpu.VMEM(shape, F32),
            pltpu.VMEM(line_xy.shape, F32),
            pltpu.VMEM(line_z.shape, F32),
            pltpu.VMEM(pieces, F32),
            pltpu.VMEM(pieces, F32),
            *[pltpu.VMEM(parts, F32)] * 10,
            pltpu.VMEM(pieces, F32),
            pltpu.VMEM(pieces, F32),
            pltpu.VMEM((2, 1024, 512), BF16),
            pltpu.VMEM((2, 2, 512, 1024), BF16),
            dma((5,)), dma((4,)), dma((4,)), dma((4, 4, 3)), dma((4, 4, 3)),
            dma((4,)), dma((4,)), dma((4,)), dma((4,)),
        ],
        compiler_params=pltpu.CompilerParams(
            collective_id=0, has_side_effects=True, vmem_limit_bytes=48 * 2**20
        ),
        name="contour_step",
    )(in_hbm(start_field), in_hbm(end_adjoint), in_hbm(potential), in_hbm(line_xy), in_hbm(line_z))
    return pl.pallas_call(
        store,
        out_shape=[jax.ShapeDtypeStruct(shape, F32)] * 3,
        in_specs=[pl.BlockSpec(memory_space=pl.ANY)] * 3,
        out_specs=[pl.BlockSpec(memory_space=pl.ANY)] * 3,
        scratch_shapes=[dma((3,))],
        compiler_params=pltpu.CompilerParams(vmem_limit_bytes=8 * 2**20),
        name="store",
    )(*[pltpu.with_memory_space_constraint(out, pltpu.VMEM) for out in outs])


def solution(mesh):
    placed = (P("px", "py", None), P("px", "py", None), P("px", "py", None), P(), P())
    return jax.shard_map(
        body,
        mesh=mesh,
        in_specs=placed,
        out_specs=(P("px", "py", None), P("px", "py", None), P("px", "py", None)),
        check_vma=False,
    )
```

```python
import functools
import jax
import jax.numpy as jnp
from jax import lax
from jax.sharding import PartitionSpec as P
from jax.experimental import pallas as pl
from jax.experimental.pallas import tpu as pltpu

MESH = pl.DeviceIdType.MESH
F32 = jnp.float32
BF16 = jnp.bfloat16
NX_CHIPS, NY_CHIPS, NZ_CHIPS = 4, 4, 16


def split(value):
    high = value.astype(BF16)
    return high, (value - high.astype(F32)).astype(BF16)


def contract(left, right, dims):
    return lax.dot_general(left, right, (dims, ((), ())), preferred_element_type=F32)


NN = ((1,), (0,))
NT = ((1,), (1,))


def stacked(value):
    return jnp.concatenate(split(value), axis=0)


def contract_left(left, right, dims):
    rows = left.shape[0] // 2
    high, low = split(right)
    both = contract(left, high, dims)
    return both[:rows] + (both[rows:] + contract(left[:rows], low, dims))


def kernel(
    start_hbm, end_hbm, potential_hbm, xy_hbm, z_hbm,
    final_out, first_out, density_out,
    field, half, pot, xy, lz,
    send_z, got_z, out_x, in_x, turn_x, home_x, in_y, part_own, part_send, part_got, turn_y, home_y, send_back, got_back,
    weight_x, weight_y,
    in_sem, z_send_sem, z_recv_sem, ring_send_sem, ring_recv_sem,
    c_send_sem, c_recv_sem, b_send_sem, b_recv_sem,
):
    px, py = lax.axis_index("px"), lax.axis_index("py")
    x, z_low = px // 8, px % 8
    y, z_high, core = py // 4, (py // 2) % 2, py % 2
    z = z_high * 8 + z_low

    def device(x_at, y_at, z_at, core_at):
        return {"px": x_at * 8 + z_at % 8, "py": y_at * 4 + (z_at // 8) * 2 + core_at}

    loads = [
        pltpu.make_async_copy(source, target, in_sem.at[i])
        for i, (source, target) in enumerate(
            [(potential_hbm, pot), (start_hbm, field.at[0]), (z_hbm, lz), (xy_hbm, xy), (end_hbm, field.at[1])]
        )
    ]
    for load in loads[:3]:
        load.start()

    barrier = pltpu.get_barrier_semaphore()

    def signal(target):
        pl.semaphore_signal(barrier, inc=1, device_id=target, device_id_type=MESH)

    @pl.loop(1, NZ_CHIPS)
    def _(step):
        signal(device(x, y, (z + step) % NZ_CHIPS, core))

    for step in range(1, 4):
        signal(device((x + step) % 4, y, z, core))
        signal(device(x, (y + step) % 4, z, core))
    signal(device(x, y, z, 1 - core))

    def exchange_z(source, target, send_sem, recv_sem, chunk, first=0):
        mine = pl.ds(pl.multiple_of(z * 32, 32), 32)

        def send(peer):
            pltpu.make_async_remote_copy(
                source.at[chunk, pl.ds(pl.multiple_of(peer * 32, 32), 32)], target.at[chunk, mine],
                send_sem.at[chunk], recv_sem.at[chunk],
                device_id=device(x, y, peer, core), device_id_type=MESH,
            ).start()

        for peer in range(first):
            @pl.when(peer != z)
            def _(peer=peer):
                send(peer)

        @pl.loop(0, NZ_CHIPS - 1)
        def _(i):
            step = NZ_CHIPS // 2 + i // 2 - (i % 2) * (2 * (i // 2) + 1)
            peer = (z + step) % NZ_CHIPS
            if first == 0:
                send(peer)
            else:
                @pl.when(peer >= first)
                def _():
                    send(peer)

        pltpu.make_async_copy(source.at[chunk, mine], target.at[chunk, mine], recv_sem.at[chunk]).start()

    def wait_z(target, recv_sem, chunk):
        pltpu.make_async_copy(target.at[chunk], target.at[chunk], recv_sem.at[chunk]).wait()

    def wait_z_sent(source, send_sem, chunk):
        sent = source.at[chunk, pl.ds(0, 480)]
        pltpu.make_async_copy(sent, sent, send_sem.at[chunk]).wait()

    exchanges = ((out_x, in_x, 0), (turn_x, home_x, 0), (home_x, in_y, 1), (turn_y, home_y, 1))

    def ring_copies(stage, chunk):
        source, target, axis = exchanges[stage]
        here = x if axis == 0 else y
        copies = []
        for step in (2, 1, 3):
            there = (here + step) % 4
            peer = device(there, y, z, core) if axis == 0 else device(x, there, z, core)
            copies.append(
                pltpu.make_async_remote_copy(
                    source.at[chunk, there], target.at[chunk, here],
                    ring_send_sem.at[chunk], ring_recv_sem.at[stage, chunk],
                    device_id=peer, device_id_type=MESH,
                )
            )
        return copies

    def ring_start(stage, chunk):
        source, target, axis = exchanges[stage]
        here = x if axis == 0 else y
        for copy in ring_copies(stage, chunk):
            copy.start()
        target[chunk, here] = source[chunk, here]

    def ring_wait(stage, chunk):
        got = exchanges[stage][1].at[chunk, pl.ds(0, 3)]
        pltpu.make_async_copy(got, got, ring_recv_sem.at[stage, chunk]).wait()

    def core_copy(chunk):
        return pltpu.make_async_remote_copy(
            part_send.at[chunk], part_got.at[chunk], c_send_sem.at[chunk], c_recv_sem.at[chunk],
            device_id=device(x, y, z, 1 - core), device_id_type=MESH,
        )

    lane = lax.broadcasted_iota(jnp.int32, (8, 128), 1)
    low_64 = lane % 128 < 64
    low_32 = lane % 64 < 32

    def regroup(a, b, c, d):
        a, c = jnp.where(low_64, a, pltpu.roll(c, 64, 1)), jnp.where(low_64, pltpu.roll(a, 64, 1), c)
        b, d = jnp.where(low_64, b, pltpu.roll(d, 64, 1)), jnp.where(low_64, pltpu.roll(b, 64, 1), d)
        a, b = jnp.where(low_32, a, pltpu.roll(b, 32, 1)), jnp.where(low_32, pltpu.roll(a, 96, 1), b)
        c, d = jnp.where(low_32, c, pltpu.roll(d, 32, 1)), jnp.where(low_32, pltpu.roll(c, 96, 1), d)
        return a, b, c, d

    def step_z(chunk, line, field_values):
        value = contract(line, field_values[0], NT)
        value = value[:128] + (value[128:] + contract(line[:128], field_values[1], NT))
        for at in range(16):
            for tile in range(4):
                send_z[chunk, pl.ds(at * 32 + tile * 8, 8)] = value[at * 8 : at * 8 + 8, tile * 128 : tile * 128 + 128]

    def step_z_send(chunk):
        exchange_z(send_z, got_z, z_send_sem, z_recv_sem, chunk)

    def step_a(chunk):
        wait_z(got_z, z_recv_sem, chunk)
        for pair in range(4):
            for tile in range(4):
                parts = [
                    got_z[chunk, pl.ds(high * 256 + tile * 8 + pair * 2 + p, 8, stride=32), :]
                    for p in range(2) for high in range(2)
                ]
                for i, part in enumerate(regroup(*parts)):
                    out_x[chunk, pair, pl.ds((tile * 4 + i) * 8, 8), :] = part
        ring_start(0, chunk)

    def step_b(chunk):
        ring_wait(0, chunk)
        values = in_x[chunk].reshape(512, 128)
        turn_x[chunk] = contract_left(weight_x[chunk // 2], values, NN).reshape(4, 128, 128)
        ring_start(1, chunk)

    def step_c(chunk):
        ring_wait(1, chunk)
        ring_start(2, chunk)

    def step_d(chunk):
        kind = chunk // 2
        ring_wait(2, chunk)
        values = stacked(jnp.concatenate([in_y[chunk, k] for k in range(4)], axis=1))
        for block in range(4):
            lanes = pl.ds(block * 256, 256)
            out = contract(values, weight_y[kind, 0, :, lanes], NN)
            out = out[:128] + (out[128:] + contract(values[:128], weight_y[kind, 1, :, lanes], NN))
            part_own[chunk, block] = out[:, :128]
            part_send[chunk, block] = out[:, 128:]
        core_copy(chunk).start()

    def step_e(chunk):
        core_copy(chunk).wait_recv()
        turn_y[chunk] = part_own[chunk] + part_got[chunk]
        ring_start(3, chunk)

    def step_f(chunk):
        ring_wait(3, chunk)
        for pair in range(4):
            for tile in range(4):
                parts = regroup(*[home_y[chunk, pair, pl.ds((tile * 4 + i) * 8, 8)] for i in range(4)])
                for p in range(2):
                    for high in range(2):
                        rows = pl.ds(high * 256 + tile * 8 + pair * 2 + p, 8, stride=32)
                        send_back[chunk, rows, :] = parts[p * 2 + high]
        exchange_z(send_back, got_back, b_send_sem, b_recv_sem, chunk, 8 if chunk == 3 else 0)

    def step_last(chunk):
        kind = chunk // 2
        lanes = pl.ds((chunk % 2) * 128, 128)
        wait_z(got_back, b_recv_sem, chunk)
        arrived = got_back[chunk].reshape(16, 4, 8, 128)
        value = jnp.concatenate(
            [jnp.transpose(arrived[:, tile].reshape(128, 128)).reshape(4, 32, 128) for tile in range(4)]
        ) * half[:, :, lanes]
        if kind == 0:
            final_out[:, :, lanes] = value
        else:
            first_out[:, :, lanes] = value
            density_out[:, :, lanes] = 0.05 * (
                field[0, :, :, lanes] * value + final_out[:, :, lanes] * field[1, :, :, lanes]
            )

    for load in loads[:3]:
        load.wait()
    for load in loads[3:]:
        load.start()
    half[...] = jnp.exp(-0.05 * pot[...])
    values = split((half[...] * field[0]).reshape(512, 256))
    step_z(0, stacked(lz[:128, :]), values)
    pl.semaphore_wait(barrier, 22)
    step_z_send(0)
    step_z(1, stacked(lz[128:, :]), values)
    step_z_send(1)

    loads[3].wait()
    loads[4].wait()
    row = lax.broadcasted_iota(jnp.int32, (128, 128), 0)
    column = lax.broadcasted_iota(jnp.int32, (128, 128), 1)
    order_x = (column == (row % 8) * 16 + row // 8).astype(F32).astype(BF16)
    order_y = (column == (row % 64) // 32 * 64 + core * 32 + row % 32).astype(F32).astype(BF16)
    row = lax.broadcasted_iota(jnp.int32, (256, 128), 0)
    column = lax.broadcasted_iota(jnp.int32, (256, 128), 1)
    other = (core + row // 128) % 2
    order_out = (column == (row % 64) // 32 * 64 + other * 32 + row % 32).astype(F32).astype(BF16)
    row = lax.broadcasted_iota(jnp.int32, (128, 256), 0)
    column = lax.broadcasted_iota(jnp.int32, (128, 256), 1)
    same = row // 64 == column % 128 // 64
    for kind in range(2):
        for k in range(4):
            block = pl.ds(k * 128, 128)
            parts = split(xy[block, :] if kind == 0 else xy[:, block])
            columns = split(xy[:, block] if kind == 0 else xy[block, :])
            for part in range(2):
                rows = pl.ds(part * 512 + k * 128, 128)
                turned = contract(order_x, parts[part], NN if kind == 0 else NT).astype(BF16)
                for i in range(4):
                    at = slice(i * 128, i * 128 + 128)
                    weight_x[kind, rows, at] = contract(turned[:, at], order_x, NT).astype(BF16)
                turned = contract(order_y, columns[part], NT if kind == 0 else NN).astype(BF16)
                for i in range(4):
                    value = contract(turned[:, i * 128 : i * 128 + 128], order_out, NT)
                    weight_y[kind, part, block, pl.ds(i * 256, 256)] = jnp.where(same, value, 0.0).astype(BF16)

    turned = jnp.transpose(lz[...])
    values = split((half[...] * field[1]).reshape(512, 256))
    step_z(2, stacked(turned[:128, :]), values)
    step_z(3, stacked(turned[128:, :]), values)

    step_z_send(2)
    step_z_send(3)
    step_a(0)
    step_b(0)
    step_c(0)
    step_a(1)
    step_d(0)
    step_b(1)
    step_e(0)
    step_c(1)
    step_f(0)
    step_a(2)
    step_d(1)
    step_e(1)
    step_b(2)
    step_f(1)
    step_c(2)
    step_a(3)
    step_d(2)
    step_b(3)
    step_e(2)
    step_c(3)
    step_f(2)
    step_d(3)
    step_e(3)
    step_f(3)
    for chunk in range(3):
        step_last(chunk)

    for chunk in range(4):
        wait_z_sent(send_z, z_send_sem, chunk)
        for source in (out_x, turn_x, home_x, turn_y):
            sent = source.at[chunk, pl.ds(0, 3)]
            pltpu.make_async_copy(sent, sent, ring_send_sem.at[chunk]).wait()
        core_copy(chunk).wait_send()
        if chunk < 3:
            wait_z_sent(send_back, b_send_sem, chunk)
    step_last(3)
    wait_z_sent(send_back, b_send_sem, 3)


def store(*refs):
    sources, targets, sem = refs[:3], refs[3:6], refs[6]
    copies = [pltpu.make_async_copy(a, b, sem.at[i]) for i, (a, b) in enumerate(zip(sources, targets))]
    for copy in copies:
        copy.start()
    for copy in copies:
        copy.wait()


def in_hbm(array):
    return pltpu.with_memory_space_constraint(array, pltpu.HBM)


def body(start_field, end_adjoint, potential, line_xy, line_z):
    shape = start_field.shape
    dma = pltpu.SemaphoreType.DMA
    pieces = (4, 512, 128)
    parts = (4, 4, 128, 128)
    outs = pl.pallas_call(
        kernel,
        out_shape=[jax.ShapeDtypeStruct(shape, F32)] * 3,
        in_specs=[pl.BlockSpec(memory_space=pl.ANY)] * 5,
        out_specs=[pl.BlockSpec(memory_space=pltpu.VMEM)] * 3,
        scratch_shapes=[
            pltpu.VMEM((2,) + shape, F32),
            pltpu.VMEM(shape, F32),
            pltpu.VMEM(shape, F32),
            pltpu.VMEM(line_xy.shape, F32),
            pltpu.VMEM(line_z.shape, F32),
            pltpu.VMEM(pieces, F32),
            pltpu.VMEM(pieces, F32),
            *[pltpu.VMEM(parts, F32)] * 10,
            pltpu.VMEM(pieces, F32),
            pltpu.VMEM(pieces, F32),
            pltpu.VMEM((2, 1024, 512), BF16),
            pltpu.VMEM((2, 2, 512, 1024), BF16),
            dma((5,)), dma((4,)), dma((4,)), dma((4,)), dma((4, 4)),
            dma((4,)), dma((4,)), dma((4,)), dma((4,)),
        ],
        compiler_params=pltpu.CompilerParams(
            collective_id=0, has_side_effects=True, vmem_limit_bytes=48 * 2**20
        ),
        name="contour_step",
    )(in_hbm(start_field), in_hbm(end_adjoint), in_hbm(potential), in_hbm(line_xy), in_hbm(line_z))
    return pl.pallas_call(
        store,
        out_shape=[jax.ShapeDtypeStruct(shape, F32)] * 3,
        in_specs=[pl.BlockSpec(memory_space=pl.ANY)] * 3,
        out_specs=[pl.BlockSpec(memory_space=pl.ANY)] * 3,
        scratch_shapes=[dma((3,))],
        compiler_params=pltpu.CompilerParams(vmem_limit_bytes=8 * 2**20),
        name="store",
    )(*[pltpu.with_memory_space_constraint(out, pltpu.VMEM) for out in outs])


def solution(mesh):
    placed = (P("px", "py", None), P("px", "py", None), P("px", "py", None), P(), P())
    return jax.shard_map(
        body,
        mesh=mesh,
        in_specs=placed,
        out_specs=(P("px", "py", None), P("px", "py", None), P("px", "py", None)),
        check_vma=False,
    )
```

```python
import functools
import jax
import jax.numpy as jnp
from jax import lax
from jax.sharding import PartitionSpec as P
from jax.experimental import pallas as pl
from jax.experimental.pallas import tpu as pltpu

MESH = pl.DeviceIdType.MESH
F32 = jnp.float32
BF16 = jnp.bfloat16
NX_CHIPS, NY_CHIPS, NZ_CHIPS = 4, 4, 16


def split(value):
    high = value.astype(BF16)
    return high, (value - high.astype(F32)).astype(BF16)


def contract(left, right, dims):
    return lax.dot_general(left, right, (dims, ((), ())), preferred_element_type=F32)


NN = ((1,), (0,))
NT = ((1,), (1,))


def stacked(value):
    return jnp.concatenate(split(value), axis=0)


def contract_left(left, right, dims):
    rows = left.shape[0] // 2
    high, low = split(right)
    both = contract(left, high, dims)
    return both[:rows] + (both[rows:] + contract(left[:rows], low, dims))


def kernel(
    start_hbm, end_hbm, potential_hbm, xy_hbm, z_hbm,
    final_out, first_out, density_out,
    field, half, pot, xy, lz,
    send_z, got_z, out_x, in_x, turn_x, home_x, in_y, part_own, part_send, part_got, turn_y, home_y, send_back, got_back,
    weight_x, weight_y,
    in_sem, z_send_sem, z_recv_sem, ring_send_sem, ring_recv_sem,
    c_send_sem, c_recv_sem, b_send_sem, b_recv_sem,
):
    px, py = lax.axis_index("px"), lax.axis_index("py")
    x, z_low = px // 8, px % 8
    y, z_high, core = py // 4, (py // 2) % 2, py % 2
    z = z_high * 8 + z_low

    def device(x_at, y_at, z_at, core_at):
        return {"px": x_at * 8 + z_at % 8, "py": y_at * 4 + (z_at // 8) * 2 + core_at}

    pairs = [(potential_hbm, pot), (start_hbm, field.at[0]), (z_hbm, lz), (xy_hbm, xy), (end_hbm, field.at[1])]

    def load_start(i):
        source, target = pairs[i]
        rows = source.shape[0] // 4
        for piece in range(4):
            at = pl.ds(piece * rows, rows)
            pltpu.make_async_copy(source.at[at], target.at[at], in_sem.at[i]).start()

    def load_wait(i):
        pltpu.make_async_copy(pairs[i][0], pairs[i][1], in_sem.at[i]).wait()

    for i in range(3):
        load_start(i)

    barrier = pltpu.get_barrier_semaphore()

    def signal(target):
        pl.semaphore_signal(barrier, inc=1, device_id=target, device_id_type=MESH)

    @pl.loop(1, NZ_CHIPS)
    def _(step):
        signal(device(x, y, (z + step) % NZ_CHIPS, core))

    for step in range(1, 4):
        signal(device((x + step) % 4, y, z, core))
        signal(device(x, (y + step) % 4, z, core))
    signal(device(x, y, z, 1 - core))

    def exchange_z(source, target, send_sem, recv_sem, chunk, first=0):
        mine = pl.ds(pl.multiple_of(z * 32, 32), 32)

        def send(peer):
            pltpu.make_async_remote_copy(
                source.at[chunk, pl.ds(pl.multiple_of(peer * 32, 32), 32)], target.at[chunk, mine],
                send_sem.at[chunk], recv_sem.at[chunk],
                device_id=device(x, y, peer, core), device_id_type=MESH,
            ).start()

        for peer in range(first):
            @pl.when(peer != z)
            def _(peer=peer):
                send(peer)

        @pl.loop(0, NZ_CHIPS - 1)
        def _(i):
            step = NZ_CHIPS // 2 + i // 2 - (i % 2) * (2 * (i // 2) + 1)
            peer = (z + step) % NZ_CHIPS
            if first == 0:
                send(peer)
            else:
                @pl.when(peer >= first)
                def _():
                    send(peer)

        pltpu.make_async_copy(source.at[chunk, mine], target.at[chunk, mine], recv_sem.at[chunk]).start()

    def wait_z(target, recv_sem, chunk):
        pltpu.make_async_copy(target.at[chunk], target.at[chunk], recv_sem.at[chunk]).wait()

    def wait_z_sent(source, send_sem, chunk):
        sent = source.at[chunk, pl.ds(0, 480)]
        pltpu.make_async_copy(sent, sent, send_sem.at[chunk]).wait()

    exchanges = ((out_x, in_x, 0), (turn_x, home_x, 0), (home_x, in_y, 1), (turn_y, home_y, 1))

    def ring_copies(stage, chunk):
        source, target, axis = exchanges[stage]
        here = x if axis == 0 else y
        copies = []
        for step in (2, 1, 3):
            there = (here + step) % 4
            peer = device(there, y, z, core) if axis == 0 else device(x, there, z, core)
            copies.append(
                pltpu.make_async_remote_copy(
                    source.at[chunk, there], target.at[chunk, here],
                    ring_send_sem.at[chunk], ring_recv_sem.at[stage, chunk],
                    device_id=peer, device_id_type=MESH,
                )
            )
        return copies

    def ring_start(stage, chunk):
        source, target, axis = exchanges[stage]
        here = x if axis == 0 else y
        for copy in ring_copies(stage, chunk):
            copy.start()
        target[chunk, here] = source[chunk, here]

    def ring_wait(stage, chunk):
        got = exchanges[stage][1].at[chunk, pl.ds(0, 3)]
        pltpu.make_async_copy(got, got, ring_recv_sem.at[stage, chunk]).wait()

    def core_copy(chunk):
        return pltpu.make_async_remote_copy(
            part_send.at[chunk], part_got.at[chunk], c_send_sem.at[chunk], c_recv_sem.at[chunk],
            device_id=device(x, y, z, 1 - core), device_id_type=MESH,
        )

    lane = lax.broadcasted_iota(jnp.int32, (8, 128), 1)
    low_64 = lane % 128 < 64
    low_32 = lane % 64 < 32

    def regroup(a, b, c, d):
        a, c = jnp.where(low_64, a, pltpu.roll(c, 64, 1)), jnp.where(low_64, pltpu.roll(a, 64, 1), c)
        b, d = jnp.where(low_64, b, pltpu.roll(d, 64, 1)), jnp.where(low_64, pltpu.roll(b, 64, 1), d)
        a, b = jnp.where(low_32, a, pltpu.roll(b, 32, 1)), jnp.where(low_32, pltpu.roll(a, 96, 1), b)
        c, d = jnp.where(low_32, c, pltpu.roll(d, 32, 1)), jnp.where(low_32, pltpu.roll(c, 96, 1), d)
        return a, b, c, d

    def step_z(chunk, line, field_values):
        value = contract(line, field_values[0], NT)
        value = value[:128] + (value[128:] + contract(line[:128], field_values[1], NT))
        for at in range(16):
            for tile in range(4):
                send_z[chunk, pl.ds(at * 32 + tile * 8, 8)] = value[at * 8 : at * 8 + 8, tile * 128 : tile * 128 + 128]

    def step_z_send(chunk):
        exchange_z(send_z, got_z, z_send_sem, z_recv_sem, chunk)

    def step_a(chunk):
        wait_z(got_z, z_recv_sem, chunk)
        for pair in range(4):
            for tile in range(4):
                parts = [
                    got_z[chunk, pl.ds(high * 256 + tile * 8 + pair * 2 + p, 8, stride=32), :]
                    for p in range(2) for high in range(2)
                ]
                for i, part in enumerate(regroup(*parts)):
                    out_x[chunk, pair, pl.ds((tile * 4 + i) * 8, 8), :] = part
        ring_start(0, chunk)

    def step_b(chunk):
        ring_wait(0, chunk)
        values = in_x[chunk].reshape(512, 128)
        turn_x[chunk] = contract_left(weight_x[chunk // 2], values, NN).reshape(4, 128, 128)
        ring_start(1, chunk)

    def step_c(chunk):
        ring_wait(1, chunk)
        ring_start(2, chunk)

    def step_d(chunk):
        kind = chunk // 2
        ring_wait(2, chunk)
        values = stacked(jnp.concatenate([in_y[chunk, k] for k in range(4)], axis=1))
        for block in range(4):
            lanes = pl.ds(block * 256, 256)
            out = contract(values, weight_y[kind, 0, :, lanes], NN)
            out = out[:128] + (out[128:] + contract(values[:128], weight_y[kind, 1, :, lanes], NN))
            part_own[chunk, block] = out[:, :128]
            part_send[chunk, block] = out[:, 128:]
        core_copy(chunk).start()

    def step_e(chunk):
        core_copy(chunk).wait_recv()
        turn_y[chunk] = part_own[chunk] + part_got[chunk]
        ring_start(3, chunk)

    def step_f(chunk):
        ring_wait(3, chunk)
        for pair in range(4):
            for tile in range(4):
                parts = regroup(*[home_y[chunk, pair, pl.ds((tile * 4 + i) * 8, 8)] for i in range(4)])
                for p in range(2):
                    for high in range(2):
                        rows = pl.ds(high * 256 + tile * 8 + pair * 2 + p, 8, stride=32)
                        send_back[chunk, rows, :] = parts[p * 2 + high]
        exchange_z(send_back, got_back, b_send_sem, b_recv_sem, chunk, 8 if chunk == 3 else 0)

    def step_last(chunk):
        kind = chunk // 2
        lanes = pl.ds((chunk % 2) * 128, 128)
        wait_z(got_back, b_recv_sem, chunk)
        arrived = got_back[chunk].reshape(16, 4, 8, 128)
        value = jnp.concatenate(
            [jnp.transpose(arrived[:, tile].reshape(128, 128)).reshape(4, 32, 128) for tile in range(4)]
        ) * half[:, :, lanes]
        if kind == 0:
            final_out[:, :, lanes] = value
        else:
            first_out[:, :, lanes] = value
            density_out[:, :, lanes] = 0.05 * (
                field[0, :, :, lanes] * value + final_out[:, :, lanes] * field[1, :, :, lanes]
            )

    for i in range(3):
        load_wait(i)
    for i in range(3, 5):
        load_start(i)
    half[...] = jnp.exp(-0.05 * pot[...])
    values = split((half[...] * field[0]).reshape(512, 256))
    step_z(0, stacked(lz[:128, :]), values)
    pl.semaphore_wait(barrier, 22)
    step_z_send(0)
    step_z(1, stacked(lz[128:, :]), values)
    step_z_send(1)

    load_wait(3)
    load_wait(4)
    row = lax.broadcasted_iota(jnp.int32, (128, 128), 0)
    column = lax.broadcasted_iota(jnp.int32, (128, 128), 1)
    order_x = (column == (row % 8) * 16 + row // 8).astype(F32).astype(BF16)
    order_y = (column == (row % 64) // 32 * 64 + core * 32 + row % 32).astype(F32).astype(BF16)
    row = lax.broadcasted_iota(jnp.int32, (256, 128), 0)
    column = lax.broadcasted_iota(jnp.int32, (256, 128), 1)
    other = (core + row // 128) % 2
    order_out = (column == (row % 64) // 32 * 64 + other * 32 + row % 32).astype(F32).astype(BF16)
    row = lax.broadcasted_iota(jnp.int32, (128, 256), 0)
    column = lax.broadcasted_iota(jnp.int32, (128, 256), 1)
    same = row // 64 == column % 128 // 64
    for kind in range(2):
        for k in range(4):
            block = pl.ds(k * 128, 128)
            parts = split(xy[block, :] if kind == 0 else xy[:, block])
            columns = split(xy[:, block] if kind == 0 else xy[block, :])
            for part in range(2):
                rows = pl.ds(part * 512 + k * 128, 128)
                turned = contract(order_x, parts[part], NN if kind == 0 else NT).astype(BF16)
                for i in range(4):
                    at = slice(i * 128, i * 128 + 128)
                    weight_x[kind, rows, at] = contract(turned[:, at], order_x, NT).astype(BF16)
                turned = contract(order_y, columns[part], NT if kind == 0 else NN).astype(BF16)
                for i in range(4):
                    value = contract(turned[:, i * 128 : i * 128 + 128], order_out, NT)
                    weight_y[kind, part, block, pl.ds(i * 256, 256)] = jnp.where(same, value, 0.0).astype(BF16)

    turned = jnp.transpose(lz[...])
    values = split((half[...] * field[1]).reshape(512, 256))
    step_z(2, stacked(turned[:128, :]), values)
    step_z(3, stacked(turned[128:, :]), values)

    step_z_send(2)
    step_z_send(3)
    step_a(0)
    step_b(0)
    step_c(0)
    step_a(1)
    step_d(0)
    step_b(1)
    step_e(0)
    step_c(1)
    step_f(0)
    step_a(2)
    step_d(1)
    step_b(2)
    step_e(1)
    step_f(1)
    step_c(2)
    step_a(3)
    step_d(2)
    step_b(3)
    step_e(2)
    step_c(3)
    step_f(2)
    step_d(3)
    step_e(3)
    step_f(3)
    for chunk in range(3):
        step_last(chunk)

    for chunk in range(4):
        wait_z_sent(send_z, z_send_sem, chunk)
        for source in (out_x, turn_x, home_x, turn_y):
            sent = source.at[chunk, pl.ds(0, 3)]
            pltpu.make_async_copy(sent, sent, ring_send_sem.at[chunk]).wait()
        core_copy(chunk).wait_send()
        if chunk < 3:
            wait_z_sent(send_back, b_send_sem, chunk)
    step_last(3)
    wait_z_sent(send_back, b_send_sem, 3)


def store(*refs):
    sources, targets, sem = refs[:3], refs[3:6], refs[6]
    for i in range(3):
        for piece in range(4):
            at = pl.ds(piece * 4, 4)
            pltpu.make_async_copy(sources[i].at[at], targets[i].at[at], sem.at[i]).start()
    for i in range(3):
        pltpu.make_async_copy(sources[i], targets[i], sem.at[i]).wait()


def in_hbm(array):
    return pltpu.with_memory_space_constraint(array, pltpu.HBM)


def body(start_field, end_adjoint, potential, line_xy, line_z):
    shape = start_field.shape
    dma = pltpu.SemaphoreType.DMA
    pieces = (4, 512, 128)
    parts = (4, 4, 128, 128)
    outs = pl.pallas_call(
        kernel,
        out_shape=[jax.ShapeDtypeStruct(shape, F32)] * 3,
        in_specs=[pl.BlockSpec(memory_space=pl.ANY)] * 5,
        out_specs=[pl.BlockSpec(memory_space=pltpu.VMEM)] * 3,
        scratch_shapes=[
            pltpu.VMEM((2,) + shape, F32),
            pltpu.VMEM(shape, F32),
            pltpu.VMEM(shape, F32),
            pltpu.VMEM(line_xy.shape, F32),
            pltpu.VMEM(line_z.shape, F32),
            pltpu.VMEM(pieces, F32),
            pltpu.VMEM(pieces, F32),
            *[pltpu.VMEM(parts, F32)] * 10,
            pltpu.VMEM(pieces, F32),
            pltpu.VMEM(pieces, F32),
            pltpu.VMEM((2, 1024, 512), BF16),
            pltpu.VMEM((2, 2, 512, 1024), BF16),
            dma((5,)), dma((4,)), dma((4,)), dma((4,)), dma((4, 4)),
            dma((4,)), dma((4,)), dma((4,)), dma((4,)),
        ],
        compiler_params=pltpu.CompilerParams(
            collective_id=0, has_side_effects=True, vmem_limit_bytes=48 * 2**20
        ),
        name="contour_step",
    )(in_hbm(start_field), in_hbm(end_adjoint), in_hbm(potential), in_hbm(line_xy), in_hbm(line_z))
    return pl.pallas_call(
        store,
        out_shape=[jax.ShapeDtypeStruct(shape, F32)] * 3,
        in_specs=[pl.BlockSpec(memory_space=pl.ANY)] * 3,
        out_specs=[pl.BlockSpec(memory_space=pl.ANY)] * 3,
        scratch_shapes=[dma((3,))],
        compiler_params=pltpu.CompilerParams(vmem_limit_bytes=8 * 2**20),
        name="store",
    )(*[pltpu.with_memory_space_constraint(out, pltpu.VMEM) for out in outs])


def solution(mesh):
    placed = (P("px", "py", None), P("px", "py", None), P("px", "py", None), P(), P())
    return jax.shard_map(
        body,
        mesh=mesh,
        in_specs=placed,
        out_specs=(P("px", "py", None), P("px", "py", None), P("px", "py", None)),
        check_vma=False,
    )
```
